256 devices in a mesh: outer: 8 (over x, core), inner: 32 (over z, y).
Axes of the slice: x: 4, y: 4, z: 8, core: 2. Of those that a mesh axis runs over, the one named last changes fastest.
Arguments:
- query: bfloat16 [32768, 512], P(('outer', 'inner')), may hold values from -250 to 250
- key: bfloat16 [32768, 128], P(('outer', 'inner')), may hold values from -6 to 6
- value: bfloat16 [32768, 128], P(('outer', 'inner')), may hold values from -6 to 6
- grad_out: bfloat16 [32768, 512], P(('outer', 'inner')), may hold values from -6 to 6
- stretch_order: int32 [64], replicated, may hold values from 0 to 63, each once
Outputs:
- grad_query: bfloat16 [32768, 512], P(('outer', 'inner'))
- grad_key: bfloat16 [32768, 128], P(('outer', 'inner'))
- grad_value: bfloat16 [32768, 128], P(('outer', 'inner'))
The draws below stay inside these ranges and needn't reach their ends.
Inputs may be any that keep to these rules, and one draw needn't show every extreme that they name: `stretch_order`: a permutation of the 64 blocks; the same for every group.
All inputs are finite; a program needn't handle non-finite values.
Results may differ from the reference program's by a relative error of at most 0.014.
The reference program's roundings to bfloat16 on the way count: a program that leaves them out, or rounds other values in their place, can miss the bound.
Values may be sent and summed in bfloat16 or wider, within the bound.
A program may use at most 128 MiB of HBM per device.

```python
import jax
import jax.numpy as jnp
from jax import lax

TOK_DEV = 128
HQ = 4
DH = 128
CH = 64
GROUP = 4096
SEQ = 32768
N_OUTER = 8
N_INNER = 32


def shared_keys(key):
    return jax.random.truncated_normal(jax.random.fold_in(key, 11), -6.0, 6.0, (SEQ, DH), jnp.float32)


def draw_key(key, part):
    base = shared_keys(key)
    return base.astype(jnp.bfloat16)


def draw_query(key, part):
    key = jax.random.fold_in(key, 2)
    fresh = jax.random.truncated_normal(key, -6.0, 6.0, (SEQ, HQ, DH), jnp.float32)
    return fresh.reshape(SEQ, HQ * DH).astype(jnp.bfloat16)


def shard_levels(rng, dims, cuts, smallest, largest):
    level, own = 1.0, jax.random.fold_in(rng, 6)
    for position, blocks in cuts:
        heights = jnp.exp(jax.random.uniform(jax.random.fold_in(own, position), (blocks,), jnp.float32, smallest / len(cuts), largest / len(cuts)))
        level = level * jnp.repeat(heights, dims[position] // blocks).reshape([-1 if axis == position else 1 for axis in range(len(dims))])
    return level


def noise(stream_key, extent, scale, most, cuts=(), held_as=jnp.bfloat16):
    entries = jax.random.normal(stream_key, extent, jnp.float32) * scale
    if len(cuts) > 0:
        entries = shard_levels(stream_key, extent, cuts, -0.22, 0.18) * entries
    return jnp.clip(entries, min=-most, max=most).astype(held_as)


def setup_inputs(seed: int = 0) -> dict:
    key_list = jax.random.split(jax.random.key(seed), 6)
    query = draw_query(jax.random.fold_in(key_list[5], 71), 0)
    key = draw_key(jax.random.fold_in(key_list[5], 71), 0)
    value = noise(key_list[2], (SEQ, DH), 1.0, 6.0, ((0, 256),))
    grad_out = noise(key_list[3], (SEQ, HQ * DH), 1.0, 6.0, ((0, 256),))
    stretch_order = jax.random.permutation(key_list[4], 2 * N_INNER).astype(jnp.int32)
    return dict(query=query, key=key, value=value, grad_out=grad_out, stretch_order=stretch_order)


def attend_block(queries, grads, keys, values, allowed):
    dh = keys.shape[1]
    heads = queries.shape[1] // dh
    scale = float(dh) ** -0.5
    grad_keys = jnp.zeros(keys.shape, jnp.float32)
    grad_values = jnp.zeros(values.shape, jnp.float32)
    pieces = []
    for head in range(heads):
        q_head = queries[:, head * dh:(head + 1) * dh]
        g_head = grads[:, head * dh:(head + 1) * dh]
        scores = jnp.where(allowed, jnp.dot(q_head, keys.T, preferred_element_type=jnp.float32) * scale, -jnp.inf)
        top = jnp.max(scores, axis=1, keepdims=True)
        expo = jnp.exp(scores - top)
        recip = 1.0 / jnp.sum(expo, axis=1, keepdims=True)
        probs_low = (expo * recip).astype(jnp.bfloat16)
        output = jnp.dot(probs_low, values, preferred_element_type=jnp.float32)
        delta = jnp.sum(g_head.astype(jnp.float32) * output, axis=1, keepdims=True)
        dprobs = jnp.dot(g_head, values.T, preferred_element_type=jnp.float32)
        dscore = (expo * recip * (dprobs - delta) * scale).astype(jnp.bfloat16)
        pieces.append(jnp.dot(dscore, keys, preferred_element_type=jnp.float32).astype(jnp.bfloat16))
        grad_keys = grad_keys + jnp.dot(dscore.T, q_head, preferred_element_type=jnp.float32)
        grad_values = grad_values + jnp.dot(probs_low.T, g_head, preferred_element_type=jnp.float32)
    return jnp.concatenate(pieces, axis=1), jnp.concatenate([grad_keys, grad_values], axis=1)


def reference(query, key, value, grad_out, stretch_order):
    rows = jnp.arange(SEQ, dtype=jnp.int32)
    block_index = (rows // TOK_DEV) % N_INNER
    offset = rows % TOK_DEV
    inpos = stretch_order[2 * block_index + offset // CH] * CH + offset % CH
    joined = jnp.concatenate([key, value], axis=1)
    padded = jnp.concatenate([jnp.zeros((GROUP, 2 * DH), jnp.bfloat16), joined], axis=0)
    start_acc = jnp.zeros((SEQ + GROUP, 2 * DH), jnp.float32)

    def step(acc, device):
        group = device // N_INNER
        first = (device * TOK_DEV).astype(jnp.int32)
        base = (group * GROUP).astype(jnp.int32)
        queries = lax.dynamic_slice_in_dim(query, first, TOK_DEV, 0)
        grads = lax.dynamic_slice_in_dim(grad_out, first, TOK_DEV, 0)
        both = lax.dynamic_slice_in_dim(padded, base, 2 * GROUP, 0)
        qpos = lax.dynamic_slice_in_dim(inpos, first, TOK_DEV, 0)
        kpos = lax.dynamic_slice_in_dim(inpos, base, GROUP, 0)
        earlier = jnp.broadcast_to(group > 0, (TOK_DEV, GROUP))
        allowed = jnp.concatenate([earlier, kpos[None, :] <= qpos[:, None]], axis=1)
        dq, dkv = attend_block(queries, grads, both[:, :DH], both[:, DH:], allowed)
        old = lax.dynamic_slice_in_dim(acc, base, 2 * GROUP, 0)
        acc = lax.dynamic_update_slice_in_dim(acc, old + dkv, base, 0)
        return acc, dq

    acc, dqs = lax.scan(step, start_acc, jnp.arange(N_OUTER * N_INNER, dtype=jnp.int32))
    total = acc[GROUP:]
    grad_query = dqs.reshape(SEQ, HQ * DH)
    return grad_query, total[:, :DH].astype(jnp.bfloat16), total[:, DH:].astype(jnp.bfloat16)
```

```python
import functools
import jax
import jax.numpy as jnp
from jax import lax
from jax.experimental import pallas as pl
from jax.experimental.pallas import tpu as pltpu
from jax.sharding import PartitionSpec as P

MESH = pl.DeviceIdType.MESH
BF16, F32 = jnp.bfloat16, jnp.float32
NEG = -1e30
T = 128
NY = 4
CH = 256
COMM = True


def kernel(groups, members, q_in, k_in, v_in, g_in, order, dq_out, dk_out, dv_out,
           ka, mk, va, qa, ga, kt, qx, gt, e_buf, d_buf, factor, delta, dvacc, dkacc, dqt,
           stats, dels, dvb, dkb, dqb, pdv, pdk, rdv, rdk, rdq,
           loc, s_k, r_k, s_v, r_v, s_kf, s_vf, s_q, r_q, s_g, r_g, s_st, r_st, s_de, r_de,
           s_p, r_p, s_dv, r_dv, s_dk, r_dk, s_dq, r_dq):
    nz = members // NY
    heads = qa.shape[0]
    width = NY * T
    own_rows = nz * T
    keys = 2 * own_rows
    nch = keys // CH
    scale = float(T) ** -0.5
    cexp = scale * 1.4426950408889634
    outer = lax.axis_index("outer")
    inner = lax.axis_index("inner")
    z, y = inner // NY, inner % NY

    def ypeer(d):
        return (outer, z * NY + (y + d) % NY)

    def zpeer(d):
        return (outer, ((z + d) % nz) * NY + y)

    after = ((outer + 1) % groups, inner)
    before = ((outer + groups - 1) % groups, inner)

    def rcopy(src, dst, ssem, rsem, dev):
        return pltpu.make_async_remote_copy(src_ref=src, dst_ref=dst, send_sem=ssem, recv_sem=rsem,
                                            device_id=dev, device_id_type=MESH)

    far = sorted(range(1, nz), key=lambda d: -min(d, nz - d))
    near = far[::-1]

    def slot(ref, d):
        return ref.at[pl.ds(d * T, T)]

    def head_cols(ref, h):
        return ref.at[:, pl.ds(h * T, T)]

    def k_push(d):
        return rcopy(k_in, slot(ka, nz - d), s_k.at[d], r_k.at[nz - d], zpeer(d))

    def v_push(d):
        return rcopy(v_in, slot(va, nz - d), s_v.at[d], r_v.at[nz - d], zpeer(d))

    def k_forward(d):
        return rcopy(slot(ka, d) if d else k_in, slot(ka, nz + d), s_kf.at[d], r_k.at[nz + d], after)

    def v_forward(d):
        return rcopy(slot(va, d) if d else v_in, slot(va, nz + d), s_vf.at[d], r_v.at[nz + d], after)

    def q_push(h, d):
        return rcopy(q_in.at[:, pl.ds(h * T, T)], qa.at[h, pl.ds((NY - d) * T, T)], s_q.at[h, d], r_q.at[h, NY - d], ypeer(d))

    def g_push(h, d):
        return rcopy(g_in.at[:, pl.ds(h * T, T)], ga.at[h, pl.ds((NY - d) * T, T)], s_g.at[h, d], r_g.at[h, NY - d], ypeer(d))

    def stats_push(h, d):
        return rcopy(stats.at[h, 0], stats.at[h, NY - d], s_st.at[h, d], r_st.at[h, NY - d], ypeer(d))

    def delta_push(h, d):
        return rcopy(dels.at[h, 0], dels.at[h, NY - d], s_de.at[h, d], r_de.at[h, NY - d], ypeer(d))

    def dq_push(h, d):
        return rcopy(dqb.at[h, d], rdq.at[h, NY - d], s_dq.at[h, d], r_dq.at[h, NY - d], ypeer(d))

    def dv_back():
        return rcopy(dvb.at[pl.ds(own_rows, own_rows)], pdv, s_p.at[0], r_p.at[0], before)

    def dk_back():
        return rcopy(dkb.at[pl.ds(own_rows, own_rows)], pdk, s_p.at[1], r_p.at[1], before)

    def dv_push(d):
        return rcopy(slot(dvb, d), rdv.at[nz - d], s_dv.at[d], r_dv.at[nz - d], zpeer(d))

    def dk_push(d):
        return rcopy(slot(dkb, d), rdk.at[nz - d], s_dk.at[d], r_dk.at[nz - d], zpeer(d))

    if COMM:
        peers = [ypeer(d) for d in range(1, NY)] + [zpeer(d) for d in range(1, nz)] + [after, before]
        barrier = pltpu.get_barrier_semaphore()
        for peer in peers:
            pl.semaphore_signal(barrier, inc=1, device_id=peer, device_id_type=MESH)
        pl.semaphore_wait(barrier, len(peers))
        k_forward(0).start()
        for d in far:
            k_push(d).start()
        for h in range(heads):
            for d in (2, 1, 3):
                q_push(h, d).start()
        v_forward(0).start()
        for d in far:
            v_push(d).start()
        for h in range(heads):
            for d in (2, 1, 3):
                g_push(h, d).start()
    locals_ = [
        pltpu.make_async_copy(k_in, slot(ka, 0), loc.at[0]),
        pltpu.make_async_copy(v_in, slot(va, 0), loc.at[1]),
    ]
    for h in range(heads):
        locals_.append(pltpu.make_async_copy(head_cols(q_in, h), qa.at[h, pl.ds(0, T)], loc.at[2 + 2 * h]))
        locals_.append(pltpu.make_async_copy(head_cols(g_in, h), ga.at[h, pl.ds(0, T)], loc.at[3 + 2 * h]))
    for c in locals_:
        c.start()

    nst = 2 * NY
    lane = lax.broadcasted_iota(jnp.int32, (1, T), 1)
    qorder = jnp.full((1, T), 1 << 20, jnp.int32)
    for s in range(nst):
        block = z * NY + (y + s // 2) % NY
        qorder = jnp.where(lane == s, order[2 * block + s % 2], qorder)
    for a in range(2 * nz):
        block = ((z + a // 2) % nz) * NY + y
        row = jnp.where(order[2 * block + a % 2] > qorder, NEG, 0.0)
        mk[pl.ds(a * (T // 2), T // 2), :] = jnp.broadcast_to(row, (T // 2, T)).astype(BF16)
    first = jnp.where(jnp.logical_and(outer == 0, lane < nst), NEG, 0.0)
    mk[pl.ds(own_rows, own_rows), :] = jnp.broadcast_to(first, (own_rows, T)).astype(BF16)
    sub = lax.broadcasted_iota(jnp.int32, (T, width), 0)
    col = lax.broadcasted_iota(jnp.int32, (T, width), 1)
    qx[pl.ds(T, T), :] = jnp.where(sub == col // (T // 2), 1.0, 0.0).astype(BF16)
    o0, o1 = order[2 * inner], order[2 * inner + 1]
    kt_i = lax.broadcasted_iota(jnp.int32, (T, T), 0)
    qt_i = lax.broadcasted_iota(jnp.int32, (T, T), 1)
    half = T // 2
    kpos = jnp.where(kt_i < half, o0, o1) * half + kt_i % half
    qpos = jnp.where(qt_i < half, o0, o1) * half + qt_i % half
    diag = kpos <= qpos

    for c in locals_:
        c.wait()
    if COMM:
        for d in near:
            k_push(nz - d).wait_recv()
            k_forward(d).start()
        for d in [0] + near:
            k_forward(d).wait_recv()

    def rows_of(i):
        return pl.ds(pl.multiple_of(i * CH, CH), CH)

    def stage1(h, carry):
        if COMM:
            for d in range(1, NY):
                q_push(h, d).wait_recv()
        qx[pl.ds(0, T), :] = qa[h].T

        def scores(i):
            rows = rows_of(i)
            left = jnp.concatenate([ka[rows, :], mk[rows, :]], axis=1)
            s = jnp.dot(left, qx[...], preferred_element_type=F32)
            e_buf[h, rows, :] = s
            return s

        def fold(s):
            return s.reshape(CH // 8, 8, width)

        scores(0)
        e_buf[h, pl.ds(0, T), pl.ds(0, T)] = jnp.where(diag, e_buf[h, pl.ds(0, T), pl.ds(0, T)], NEG)
        top8 = jnp.max(fold(e_buf[h, pl.ds(0, CH), :]), axis=0)
        top8 = lax.fori_loop(1, nch, lambda i, t: jnp.maximum(t, jnp.max(fold(scores(i)), axis=0)), top8)
        top = jnp.max(top8, axis=0, keepdims=True)

        def expo(i, acc):
            rows = rows_of(i)
            e = jnp.exp2((e_buf[h, rows, :] - top) * cexp)
            e_buf[h, rows, :] = e
            return acc + jnp.sum(fold(e), axis=0)

        sum8 = lax.fori_loop(0, nch, expo, jnp.zeros((8, width), F32))
        stats[h, 0, pl.ds(0, 1), :] = top
        stats[h, 0, pl.ds(1, 1), :] = jnp.sum(sum8, axis=0, keepdims=True)
        if COMM:
            for d in (2, 1, 3):
                stats_push(h, d).start()
        return carry

    lax.fori_loop(0, heads, stage1, 0)

    def aligned(ref, h, r, row):
        part = ref[h, r, pl.ds(row, 1), :]
        if r == 0:
            return part
        cut = (NY - r) * T
        return jnp.concatenate([part[:, cut:], part[:, :cut]], axis=1)

    if COMM:
        for d in near:
            v_push(nz - d).wait_recv()
            v_forward(d).start()
        for d in [0] + near:
            v_forward(d).wait_recv()
    for i in range(nch):
        kt[i] = ka[pl.ds(i * CH, CH), :].T

    def stage2(h, carry):
        if COMM:
            for d in range(1, NY):
                stats_push(h, d).wait_recv()
                g_push(h, d).wait_recv()
        tops = [aligned(stats, h, r, 0) for r in range(NY)]
        sums = [aligned(stats, h, r, 1) for r in range(NY)]
        top = functools.reduce(jnp.maximum, tops)
        weights = [jnp.exp2((t - top) * cexp) for t in tops]
        total = sum(w * s for w, s in zip(weights, sums))
        f = weights[0] * (1.0 / total)
        factor[h] = f * scale
        gt[...] = ga[h].T

        def body(i, acc):
            rows = rows_of(i)
            pb = (e_buf[h, rows, :] * f).astype(BF16)
            dp = jnp.dot(va[rows, :], gt[...], preferred_element_type=F32)
            d_buf[h, rows, :] = dp
            dvacc[rows, :] = dvacc[rows, :] + jnp.dot(pb, ga[h], preferred_element_type=F32)
            return acc + jnp.sum((pb.astype(F32) * dp).reshape(CH // 8, 8, width), axis=0)

        acc = lax.fori_loop(0, nch, body, jnp.zeros((8, width), F32))
        dels[h, 0] = jnp.sum(acc, axis=0, keepdims=True)
        if COMM:
            for d in (2, 1, 3):
                delta_push(h, d).start()
        return carry

    dvacc[...] = jnp.zeros_like(dvacc)
    dkacc[...] = jnp.zeros_like(dkacc)
    dqt[...] = jnp.zeros_like(dqt)
    lax.fori_loop(0, heads, stage2, 0)
    dvb[pl.ds(own_rows, own_rows), :] = dvacc[pl.ds(own_rows, own_rows), :].astype(BF16)
    if COMM:
        dv_back().start()

    def stage3(lo, hi, first_part, last_part):
        def run(h, carry):
            if first_part:
                if COMM:
                    for d in range(1, NY):
                        delta_push(h, d).wait_recv()
                delta[h] = sum(aligned(dels, h, r, 0) for r in range(NY))
            f, dl = factor[h], delta[h]

            def body(i, c):
                rows = rows_of(i)
                ds = ((e_buf[h, rows, :] * f) * (d_buf[h, rows, :] - dl)).astype(BF16)
                dkacc[rows, :] = dkacc[rows, :] + jnp.dot(ds, qa[h], preferred_element_type=F32)
                dqt[h] = dqt[h] + jnp.dot(kt[i], ds, preferred_element_type=F32)
                return c

            lax.fori_loop(lo // CH, hi // CH, body, 0)
            if last_part:
                for d in range(1, NY):
                    dqb[h, d] = dqt[h, :, pl.ds(d * T, T)].T.astype(BF16)
                if COMM:
                    for d in (2, 1, 3):
                        dq_push(h, d).start()
            return carry

        lax.fori_loop(0, heads, run, 0)

    mid = own_rows // 2
    stage3(own_rows, keys, True, False)
    dkb[pl.ds(own_rows, own_rows), :] = dkacc[pl.ds(own_rows, own_rows), :].astype(BF16)
    if COMM:
        dk_back().start()
        dv_back().wait_recv()
    dvacc[pl.ds(0, own_rows), :] = dvacc[pl.ds(0, own_rows), :] + pdv[...].astype(F32)
    dvb[pl.ds(0, own_rows), :] = dvacc[pl.ds(0, own_rows), :].astype(BF16)
    if COMM:
        for d in far:
            dv_push(d).start()
    stage3(mid, own_rows, False, False)
    if COMM:
        dk_back().wait_recv()
    dkb[pl.ds(mid, mid), :] = (dkacc[pl.ds(mid, mid), :] + pdk[pl.ds(mid, mid), :].astype(F32)).astype(BF16)
    if COMM:
        for d in far:
            if d * T >= mid:
                dk_push(d).start()
    stage3(0, mid, False, True)
    dkacc[pl.ds(0, mid), :] = dkacc[pl.ds(0, mid), :] + pdk[pl.ds(0, mid), :].astype(F32)
    dkb[pl.ds(0, mid), :] = dkacc[pl.ds(0, mid), :].astype(BF16)
    if COMM:
        for d in far:
            if d * T < mid:
                dk_push(d).start()

    if COMM:
        for d in far:
            dv_push(d).wait_recv()
    dv_out[...] = (dvacc[pl.ds(0, T), :] + sum(rdv[nz - d].astype(F32) for d in range(1, nz))).astype(BF16)
    for h in range(heads):
        if COMM:
            for d in range(1, NY):
                dq_push(h, d).wait_recv()
        mine = dqt[h, :, pl.ds(0, T)].T
        dq_out[:, pl.ds(h * T, T)] = (mine + sum(rdq[h, d].astype(F32) for d in range(1, NY))).astype(BF16)
    if COMM:
        for d in far:
            dk_push(d).wait_recv()
    dk_out[...] = (dkacc[pl.ds(0, T), :] + sum(rdk[nz - d].astype(F32) for d in range(1, nz))).astype(BF16)

    if COMM:
        dv_back().wait_send()
        dk_back().wait_send()
        for d in range(nz):
            k_forward(d).wait_send()
            v_forward(d).wait_send()
            if d:
                k_push(d).wait_send()
                v_push(d).wait_send()
                dv_push(d).wait_send()
                dk_push(d).wait_send()
        for h in range(heads):
            for d in range(1, NY):
                for push in (q_push, g_push, stats_push, delta_push, dq_push):
                    push(h, d).wait_send()


def fused(groups, members, query, key, value, grad_out, stretch_order):
    tokens, dh = key.shape
    heads = query.shape[1] // dh
    nz = members // NY
    own = nz * tokens
    keys, width = 2 * own, NY * tokens
    dma = pltpu.SemaphoreType.DMA
    any_spec = pl.BlockSpec(memory_space=pl.ANY)
    vm = pl.BlockSpec(memory_space=pltpu.VMEM)
    V = pltpu.VMEM
    return pl.pallas_call(
        functools.partial(kernel, groups, members),
        out_shape=(jax.ShapeDtypeStruct(query.shape, BF16), jax.ShapeDtypeStruct(key.shape, BF16),
                   jax.ShapeDtypeStruct(value.shape, BF16)),
        in_specs=[any_spec] * 4 + [pl.BlockSpec(memory_space=pltpu.SMEM)],
        out_specs=(vm, vm, vm),
        scratch_shapes=[
            V((keys, dh), BF16), V((keys, dh), BF16), V((keys, dh), BF16),
            V((heads, width, dh), BF16), V((heads, width, dh), BF16),
            V((keys // CH, dh, CH), BF16), V((2 * dh, width), BF16), V((dh, width), BF16),
            V((heads, keys, width), F32), V((heads, keys, width), F32),
            V((heads, 1, width), F32), V((heads, 1, width), F32),
            V((keys, dh), F32), V((keys, dh), F32), V((heads, dh, width), F32),
            V((heads, NY, 2, width), F32), V((heads, NY, 1, width), F32),
            V((keys, dh), BF16), V((keys, dh), BF16), V((heads, NY, tokens, dh), BF16),
            V((own, dh), BF16), V((own, dh), BF16),
            V((nz, tokens, dh), BF16), V((nz, tokens, dh), BF16), V((heads, NY, tokens, dh), BF16),
            dma((2 + 2 * heads,)),
            dma((nz,)), dma((2 * nz,)), dma((nz,)), dma((2 * nz,)), dma((nz,)), dma((nz,)),
            dma((heads, NY)), dma((heads, NY)), dma((heads, NY)), dma((heads, NY)),
            dma((heads, NY)), dma((heads, NY)), dma((heads, NY)), dma((heads, NY)),
            dma((2,)), dma((2,)), dma((nz,)), dma((nz,)), dma((nz,)), dma((nz,)),
            dma((heads, NY)), dma((heads, NY)),
        ],
        name="attention_backward",
        compiler_params=pltpu.CompilerParams(
            **(dict(collective_id=0, has_side_effects=True) if COMM else {}), vmem_limit_bytes=60 << 20),
    )(query, key, value, grad_out, stretch_order)


def solution(mesh):
    groups, members = mesh.shape["outer"], mesh.shape["inner"]
    spec = P(("outer", "inner"), None)
    return jax.shard_map(
        functools.partial(fused, groups, members), mesh=mesh,
        in_specs=(spec, spec, spec, spec, P()), out_specs=(spec, spec, spec), check_vma=False)
```

```python
import functools
import jax
import jax.numpy as jnp
from jax import lax
from jax.experimental import pallas as pl
from jax.experimental.pallas import tpu as pltpu
from jax.sharding import PartitionSpec as P

MESH = pl.DeviceIdType.MESH
BF16, F32 = jnp.bfloat16, jnp.float32
NEG = -1e30
T = 128
NY = 4
CS = 256
CC = 1024
CD = 512
COMM = True
TN = 0
BARZ = (1, 2, 6, 7)
BARY = (1, 3)


def kernel(groups, members, q_in, k_in, v_in, g_in, order, dq_out, dk_out, dv_out,
           ka, mk, va, qa, ga, kt, qx, gx, e_buf, d_buf, dvacc, dkacc, dqt,
           stats, dels, tops8, sums8, dvb, dkb, dvp, dkp, dqb, pdv, pdk, rdv, rdk, rdvp, rdkp, rdq,
           loc, s_k, r_k, s_v, r_v, s_kf, s_vf, s_q, r_q, s_g, r_g, s_st, r_st, s_de, r_de,
           s_p, r_p, s_dv, r_dv, s_dk, r_dk, s_dvp, r_dvp, s_dkp, r_dkp, s_dq, r_dq):
    nz = members // NY
    heads = qa.shape[0]
    width = NY * T
    own_rows = nz * T
    keys = 2 * own_rows
    scale = float(T) ** -0.5
    cexp = scale * 1.4426950408889634
    outer = lax.axis_index("outer")
    inner = lax.axis_index("inner")
    z, y = inner // NY, inner % NY
    after = ((outer + 1) % groups, inner)
    before = ((outer + groups - 1) % groups, inner)
    near = sorted(range(1, nz), key=lambda d: (min(d, nz - d), d))
    far = near[::-1]
    place = {d: i for i, d in enumerate([0] + near)}
    ydist = (2, 1, 3)
    mid = nz // 2

    def ypeer(d):
        return (outer, z * NY + (y + d) % NY)

    def zpeer(d):
        return (outer, ((z + d) % nz) * NY + y)

    def at(ref, d, prior=False):
        return ref.at[pl.ds(place[d] * T + (own_rows if prior else 0), T)]

    def cols(ref, h):
        return ref.at[:, pl.ds(h * T, T)]

    def copy_of(kind, h, d):
        if kind in ("k", "v"):
            ref, src, ssem, rsem = (ka, k_in, s_k, r_k) if kind == "k" else (va, v_in, s_v, r_v)
            s, e = h
            return (at(ref, s) if s else src, at(ref, d), ssem.at[d], rsem.at[d], zpeer(e))
        if kind in ("kf", "vf"):
            ref, src, ssem, rsem = (ka, k_in, s_kf, r_k) if kind == "kf" else (va, v_in, s_vf, r_v)
            return (at(ref, d) if d else src, at(ref, d, True), ssem.at[d], rsem.at[nz + d], after)
        if kind == "q":
            return (cols(q_in, h), qa.at[h, pl.ds((NY - d) * T, T)], s_q.at[h, d], r_q.at[h, NY - d], ypeer(d))
        if kind == "g":
            return (cols(g_in, h), ga.at[h, pl.ds((NY - d) * T, T)], s_g.at[h, d], r_g.at[h, NY - d], ypeer(d))
        if kind in ("qr", "gr"):
            ref, ssem, rsem = (qa, s_q, r_q) if kind == "qr" else (ga, s_g, r_g)
            return (ref.at[h, pl.ds((NY - d) * T, T)], ref.at[h, pl.ds(2 * T, T)], ssem.at[h, 2], rsem.at[h, 2], ypeer(d))
        if kind == "stats":
            return (stats.at[h, 0], stats.at[h, NY - d], s_st.at[h, d], r_st.at[h, NY - d], ypeer(d))
        if kind == "delta":
            return (dels.at[h, 0], dels.at[h, NY - d], s_de.at[h, d], r_de.at[h, NY - d], ypeer(d))
        if kind == "dq":
            return (dqb.at[h, d], rdq.at[h, NY - d], s_dq.at[h, d], r_dq.at[h, NY - d], ypeer(d))
        if kind in ("pdv", "pdk"):
            src, dst = (dvacc, pdv) if kind == "pdv" else (dkacc, pdk)
            i = d + (2 if kind == "pdk" else 0)
            return (src.at[pl.ds(own_rows + d * mid * T, mid * T)], dst.at[pl.ds(d * mid * T, mid * T)],
                    s_p.at[i], r_p.at[i], before)
        if kind in ("dvp", "dkp"):
            src, dst, ssem, rsem = (dvp, rdvp, s_dvp, r_dvp) if kind == "dvp" else (dkp, rdkp, s_dkp, r_dkp)
            return (at(src, d), dst.at[(nz - d) % nz], ssem.at[d], rsem.at[(nz - d) % nz],
                    (before[0], ((z + d) % nz) * NY + y))
        if kind == "dv":
            return (at(dvb, d), rdv.at[nz - d], s_dv.at[d], r_dv.at[nz - d], zpeer(d))
        return (at(dkb, d), rdk.at[nz - d], s_dk.at[d], r_dk.at[nz - d], zpeer(d))

    started, received = [], set()

    def remote(key):
        src, dst, ssem, rsem, dev = copy_of(*key)
        return pltpu.make_async_remote_copy(src_ref=src, dst_ref=dst, send_sem=ssem, recv_sem=rsem,
                                            device_id=dev, device_id_type=MESH)

    def start(kind, h=0, ds=(0,)):
        for d in ds:
            started.append((kind, h, d))
            if COMM:
                remote((kind, h, d)).start()

    def recv(kind, h=0, ds=(0,)):
        for d in ds:
            if (kind, h, d) in received:
                continue
            received.add((kind, h, d))
            if COMM:
                remote((kind, h, d)).wait_recv()

    def ring_start(kind, s, steps):
        for e in steps:
            start(kind, (s, e % nz), ((s - e) % nz,))

    def ring_recv(kind, ds):
        for d in ds:
            recv(kind, (0, nz - d), (d,))

    def on_core(core, work):
        if COMM:
            pl.when(outer % 2 == core)(work)
        elif core == 1:
            work()

    def finish():
        if COMM:
            for key in started:
                remote(key).wait_send()

    locals_ = [pltpu.make_async_copy(k_in, at(ka, 0), loc.at[0]), pltpu.make_async_copy(v_in, at(va, 0), loc.at[1])]
    for h in range(heads):
        locals_.append(pltpu.make_async_copy(cols(q_in, h), qa.at[h, pl.ds(0, T)], loc.at[2 + 2 * h]))
        locals_.append(pltpu.make_async_copy(cols(g_in, h), ga.at[h, pl.ds(0, T)], loc.at[3 + 2 * h]))
    for c in locals_:
        c.start()
    if COMM:
        peers = [ypeer(d) for d in BARY] + [zpeer(d) for d in BARZ] + [after, before]
        barrier = pltpu.get_barrier_semaphore()
        for peer in peers:
            pl.semaphore_signal(barrier, inc=1, device_id=peer, device_id_type=MESH)
        pl.semaphore_wait(barrier, len(peers))
    two, six = 2, nz - 2
    ring_start("k", 0, (2, -2, 1, -1))
    start("kf")
    for h in range(heads):
        start("q", h, (1, 3))

    def start_vg():
        ring_start("v", 0, (2, -2, 1, -1))
        start("vf")
        for h in range(heads):
            start("g", h, (1, 3))

    nst = 2 * NY
    half = T // 2
    lane = lax.broadcasted_iota(jnp.int32, (1, T), 1)
    qorder = jnp.full((1, T), 1 << 20, jnp.int32)
    for s in range(nst):
        block = z * NY + (y + s // 2) % NY
        qorder = jnp.where(lane == s, order[2 * block + s % 2], qorder)
    for d in range(nz):
        block = ((z + d) % nz) * NY + y
        for i in range(2):
            row = jnp.where(order[2 * block + i] > qorder, NEG, 0.0)
            mk[pl.ds(place[d] * T + i * half, half), :] = jnp.broadcast_to(row, (half, T)).astype(BF16)
    first = jnp.where(jnp.logical_and(outer == 0, lane < nst), NEG, 0.0)
    mk[pl.ds(own_rows, own_rows), :] = jnp.broadcast_to(first, (own_rows, T)).astype(BF16)
    sub = lax.broadcasted_iota(jnp.int32, (T, width), 0)
    col = lax.broadcasted_iota(jnp.int32, (T, width), 1)
    onehot = jnp.where(sub == col // half, 1.0, 0.0).astype(BF16)
    for h in range(heads):
        qx[h, pl.ds(T, T), :] = onehot
    o0, o1 = order[2 * inner], order[2 * inner + 1]
    kt_i = lax.broadcasted_iota(jnp.int32, (T, T), 0)
    qt_i = lax.broadcasted_iota(jnp.int32, (T, T), 1)
    kpos = jnp.where(kt_i < half, o0, o1) * half + kt_i % half
    qpos = jnp.where(qt_i < half, o0, o1) * half + qt_i % half
    dvacc[...] = jnp.zeros_like(dvacc)
    dkacc[...] = jnp.zeros_like(dkacc)
    dqt[...] = jnp.zeros_like(dqt)

    for c in locals_:
        c.wait()

    def fold(x):
        return x.reshape(x.shape[0] // 8, 8, width)

    tops, sums = {}, {}

    def pass_a(h, lo, hi):
        lo, hi = lo * T, hi * T
        if lo == 0:
            recv("qr", h, turn(h))
            qx[h, pl.ds(0, T), :] = qa[h].T
        rows = pl.ds(lo, hi - lo)
        left = jnp.concatenate([ka[rows, :], mk[rows, :]], axis=1)
        s = jnp.dot(left, qx[h], preferred_element_type=F32)
        if lo == 0:
            t = jnp.where(kpos <= qpos, s[:T, :T], NEG)
            s = jnp.concatenate([jnp.concatenate([t, s[:T, T:]], axis=1), s[T:]], axis=0)
        e_buf[h, rows, :] = s
        m = jnp.max(fold(s), axis=0)
        tops8[h] = m if lo == 0 else jnp.maximum(tops8[h], m)

    def exponentials(h):
        top = jnp.max(tops8[h], axis=0, keepdims=True)
        l = jnp.zeros((8, width), F32)
        for i in range(keys // CS):
            rows = pl.ds(i * CS, CS)
            e = jnp.exp2((e_buf[h, rows, :] - top) * cexp)
            e_buf[h, rows, :] = e
            l = l + jnp.sum(fold(e), axis=0)
        stats[h, 0, pl.ds(0, 1), :] = top
        stats[h, 0, pl.ds(1, 1), :] = jnp.sum(l, axis=0, keepdims=True)
        start("stats", h, ydist)

    def prepare(h):
        recv("gr", h, turn(h))
        g = ga[h].T.astype(F32) * scale
        g_hi = g.astype(BF16)
        gx[h, pl.ds(0, T), :] = g_hi
        gx[h, pl.ds(T, T), :] = (g - g_hi.astype(F32)).astype(BF16)

    def dprobs(h, lo):
        rows = pl.ds(lo, own_rows)
        v = va[rows, :]
        d_buf[h, rows, :] = jnp.dot(jnp.concatenate([v, v], axis=1), gx[h], preferred_element_type=F32)

    def turn(h):
        return (3,) if h % 2 == 0 else (1,)

    def each_head(work, h0=0, h1=None):
        h1 = heads if h1 is None else h1
        for h in range(h0, h1):
            work(h)

    def wait_y(kind, h):
        if COMM:
            for d in ydist:
                remote((kind, h, d)).wait_recv()

    def forward(kind, ds):
        ring_recv(kind, ds)
        start(kind + "f", 0, ds)

    def relay(kind):
        for h in range(heads):
            recv(kind, h, (1, 3))
            start(kind + "r", h, turn(h))

    ring_recv("k", (six, two))
    ring_start("k", six, (1,))
    ring_start("k", two, (-1, -2))
    start("kf", 0, (six, two))
    relay("q")
    forward("k", (nz - 1, 1))
    start_vg()
    for h in range(heads):
        pass_a(h, 0, 5)
    forward("k", (3, nz - 3, mid))
    ring_recv("v", (six, two))
    ring_start("v", two, (-1,))
    ring_start("v", six, (1, 2))
    relay("g")
    start("vf", 0, (six, two))
    forward("v", (1, nz - 1))
    for h in range(heads):
        pass_a(h, 5, 8)
    recv("kf", 0, (0, 1, nz - 1, two, six))
    for h in range(heads):
        pass_a(h, 8, 13)
    forward("v", (3, nz - 3, mid))
    recv("kf", 0, (3, nz - 3, mid))
    for h in range(heads):
        pass_a(h, 13, 16)
    for h in range(heads):
        exponentials(h)
    for h in range(heads):
        prepare(h)
    for i in range(keys // CD):
        kt[i] = ka[pl.ds(i * CD, CD), :].T
    for h in range(heads):
        dprobs(h, 0)
    recv("vf", 0, [0] + near)
    for h in range(heads):
        dprobs(h, own_rows)

    def aligned(ref, h, r, row):
        part = ref[h, r, pl.ds(row, 1), :]
        if r == 0:
            return part
        cut = (NY - r) * T
        return jnp.concatenate([part[:, cut:], part[:, :cut]], axis=1)

    def second(h):
        wait_y("stats", h)
        parts = [aligned(stats, h, r, 0) for r in range(NY)]
        top = functools.reduce(jnp.maximum, parts)
        weights = [jnp.exp2((t - top) * cexp) for t in parts]
        total = sum(w * aligned(stats, h, r, 1) for r, w in enumerate(weights))
        f = weights[0] * (1.0 / total)
        acc = jnp.zeros((8, width), F32)
        for i in range(keys // CC):
            rows = pl.ds(i * CC, CC)
            p = e_buf[h, rows, :] * f
            e_buf[h, rows, :] = p
            pb = p.astype(BF16)
            dvacc[rows, :] = dvacc[rows, :] + jnp.dot(pb, ga[h], preferred_element_type=F32)
            acc = acc + jnp.sum(fold(pb.astype(F32) * d_buf[h, rows, :]), axis=0)
        dels[h, 0] = jnp.sum(acc, axis=0, keepdims=True)
        if COMM:
            for d in ydist:
                remote(("delta", h, d)).start()

    each_head(second)
    for h in range(heads):
        started.extend([("delta", h, d) for d in ydist])
    own = pl.ds(0, own_rows)
    prior = pl.ds(own_rows, own_rows)

    def each(kind, ds, act):
        if COMM:
            for d in ds:
                getattr(remote((kind, 0, d)), act)()

    @functools.partial(on_core, 0)
    def _():
        dvp[...] = dvacc[prior, :].astype(BF16)
        each("dvp", [0] + far, "start")

    @functools.partial(on_core, 1)
    def _():
        each("pdv", (0, 1), "start")
        dvb[...] = dvacc[own, :].astype(BF16)
        each("dv", far, "start")

    def dq_part(h, d):
        return dqt[h, pl.ds(d * T, T), :] if TN else dqt[h, :, pl.ds(d * T, T)].T

    def third(h, lo, n, first, last):
        if first:
            wait_y("delta", h)
        delta = sum(aligned(dels, h, r, 0) for r in range(NY))
        dq = None
        for i in range(lo * T // CD, (lo + n) * T // CD):
            rows = pl.ds(i * CD, CD)
            ds = (e_buf[h, rows, :] * (d_buf[h, rows, :] - delta)).astype(BF16)
            dkacc[rows, :] = dkacc[rows, :] + jnp.dot(ds, qa[h], preferred_element_type=F32)
            if TN:
                term = lax.dot_general(ds, ka[rows, :], (((0,), (0,)), ((), ())), preferred_element_type=F32)
            else:
                term = jnp.dot(kt[i], ds, preferred_element_type=F32)
            dq = term if dq is None else dq + term
        dqt[h] = dq if first else dqt[h] + dq
        if last:
            for d in ydist:
                dqb[h, d] = dq_part(h, d).astype(BF16)
            if COMM:
                for d in ydist:
                    remote(("dq", h, d)).start()

    def part_of(i):
        return [d for d in [0] + far if place[d] // mid == i]

    def prior_dk(i):
        rows, mine = pl.ds(own_rows + i * mid * T, mid * T), pl.ds(i * mid * T, mid * T)

        @functools.partial(on_core, 0)
        def _():
            dkp[mine, :] = dkacc[rows, :].astype(BF16)
            each("dkp", part_of(i), "start")

        @functools.partial(on_core, 1)
        def _():
            each("pdk", (i,), "start")

    def own_dk(i):
        mine = pl.ds(i * mid * T, mid * T)

        @functools.partial(on_core, 0)
        def _():
            each("pdk", (i,), "wait_recv")
            dkacc[mine, :] = dkacc[mine, :] + pdk[mine, :]

        dkb[mine, :] = dkacc[mine, :].astype(BF16)
        each("dk", [d for d in part_of(i) if d], "start")

    each_head(lambda h: third(h, nz + mid, mid, True, False))
    prior_dk(1)
    each_head(lambda h: third(h, nz, mid, False, False))
    prior_dk(0)

    @functools.partial(on_core, 0)
    def _():
        each("pdv", (0, 1), "wait_recv")
        dvacc[own, :] = dvacc[own, :] + pdv[...]
        dvb[...] = dvacc[own, :].astype(BF16)
        each("dv", far, "start")

    each_head(lambda h: third(h, mid, mid, False, False))
    own_dk(1)
    each_head(lambda h: third(h, 0, mid, False, True))
    own_dk(0)

    me = pl.ds(0, T)
    each("dv", far, "wait_recv")
    dvacc[me, :] = dvacc[me, :] + sum(rdv[d].astype(F32) for d in range(1, nz))
    for h in range(heads):
        wait_y("dq", h)
        dq_out[:, pl.ds(h * T, T)] = (dq_part(h, 0) + sum(rdq[h, d].astype(F32) for d in range(1, NY))).astype(BF16)
    each("dk", far, "wait_recv")
    dkacc[me, :] = dkacc[me, :] + sum(rdk[d].astype(F32) for d in range(1, nz))

    @functools.partial(on_core, 1)
    def _():
        each("dvp", [0] + far, "wait_recv")
        each("dkp", [0] + far, "wait_recv")
        dvacc[me, :] = dvacc[me, :] + sum(rdvp[d].astype(F32) for d in range(nz))
        dkacc[me, :] = dkacc[me, :] + sum(rdkp[d].astype(F32) for d in range(nz))

    dv_out[...] = dvacc[me, :].astype(BF16)
    dk_out[...] = dkacc[me, :].astype(BF16)
    finish()
    each("dv", far, "wait_send")
    each("dk", far, "wait_send")
    for h in range(heads):
        each_y = [remote(("dq", h, d)) for d in ydist]
        for c in each_y if COMM else []:
            c.wait_send()

    @functools.partial(on_core, 0)
    def _():
        each("dvp", [0] + far, "wait_send")
        each("dkp", [0] + far, "wait_send")

    @functools.partial(on_core, 1)
    def _():
        each("pdv", (0, 1), "wait_send")
        each("pdk", (0, 1), "wait_send")


def fused(groups, members, query, key, value, grad_out, stretch_order):
    tokens, dh = key.shape
    heads = query.shape[1] // dh
    nz = members // NY
    own = nz * tokens
    keys, width = 2 * own, NY * tokens
    dma = pltpu.SemaphoreType.DMA
    any_spec = pl.BlockSpec(memory_space=pl.ANY)
    vm = pl.BlockSpec(memory_space=pltpu.VMEM)
    V = pltpu.VMEM
    results = pl.pallas_call(
        functools.partial(kernel, groups, members),
        out_shape=(jax.ShapeDtypeStruct(query.shape, BF16), jax.ShapeDtypeStruct(key.shape, BF16),
                   jax.ShapeDtypeStruct(value.shape, BF16)),
        in_specs=[any_spec] * 4 + [pl.BlockSpec(memory_space=pltpu.SMEM)],
        out_specs=(vm, vm, vm),
        scratch_shapes=[
            V((keys, dh), BF16), V((keys, dh), BF16), V((keys, dh), BF16),
            V((heads, width, dh), BF16), V((heads, width, dh), BF16),
            V((keys // CD, dh, CD), BF16), V((heads, 2 * dh, width), BF16), V((heads, 2 * dh, width), BF16),
            V((heads, keys, width), F32), V((heads, keys, width), F32),
            V((keys, dh), F32), V((keys, dh), F32),
            V((heads, width, dh) if TN else (heads, dh, width), F32),
            V((heads, NY, 2, width), F32), V((heads, NY, 1, width), F32),
            V((heads, 8, width), F32), V((heads, 8, width), F32),
            V((own, dh), BF16), V((own, dh), BF16), V((own, dh), BF16), V((own, dh), BF16),
            V((heads, NY, tokens, dh), BF16),
            V((own, dh), F32), V((own, dh), F32),
            V((nz, tokens, dh), BF16), V((nz, tokens, dh), BF16), V((nz, tokens, dh), BF16), V((nz, tokens, dh), BF16),
            V((heads, NY, tokens, dh), BF16),
            dma((2 + 2 * heads,)),
            dma((nz,)), dma((2 * nz,)), dma((nz,)), dma((2 * nz,)), dma((nz,)), dma((nz,)),
            dma((heads, NY)), dma((heads, NY)), dma((heads, NY)), dma((heads, NY)),
            dma((heads, NY)), dma((heads, NY)), dma((heads, NY)), dma((heads, NY)),
            dma((4,)), dma((4,)),
            dma((nz,)), dma((nz,)), dma((nz,)), dma((nz,)), dma((nz,)), dma((nz,)), dma((nz,)), dma((nz,)),
            dma((heads, NY)), dma((heads, NY)),
        ],
        name="attention_backward",
        compiler_params=pltpu.CompilerParams(
            **(dict(collective_id=0, has_side_effects=True) if COMM else {}), vmem_limit_bytes=60 << 20),
    )(query, key, value, grad_out, stretch_order)
    return results


def solution(mesh):
    groups, members = mesh.shape["outer"], mesh.shape["inner"]
    spec = P(("outer", "inner"), None)
    return jax.shard_map(
        functools.partial(fused, groups, members), mesh=mesh,
        in_specs=(spec, spec, spec, spec, P()), out_specs=(spec, spec, spec), check_vma=False)
```

```python
import functools
import jax
import jax.numpy as jnp
from jax import lax
from jax.experimental import pallas as pl
from jax.experimental.pallas import tpu as pltpu
from jax.sharding import PartitionSpec as P

MESH = pl.DeviceIdType.MESH
BF16, F32 = jnp.bfloat16, jnp.float32
NEG = -1e30
T = 128
NY = 4
CS = 256
CC = 1024
CD = 512
COMM = True
TN = 0
BARZ = (1, 2, 6, 7)
BARY = (1, 2, 3)


def kernel(groups, members, q_in, k_in, v_in, g_in, order, dq_out, dk_out, dv_out,
           ka, mk, va, qa, ga, kt, qx, gx, e_buf, d_buf, dvacc, dkacc, dqt,
           stats, dels, tops8, sums8, dvb, dkb, dvp, dkp, dqb, pdv, pdk, rdv, rdk, rdvp, rdkp, rdq,
           loc, s_k, r_k, s_v, r_v, s_kf, s_vf, s_q, r_q, s_g, r_g, s_st, r_st, s_de, r_de,
           s_p, r_p, s_dv, r_dv, s_dk, r_dk, s_dvp, r_dvp, s_dkp, r_dkp, s_dq, r_dq):
    nz = members // NY
    heads = qa.shape[0]
    width = NY * T
    own_rows = nz * T
    keys = 2 * own_rows
    scale = float(T) ** -0.5
    cexp = scale * 1.4426950408889634
    outer = lax.axis_index("outer")
    inner = lax.axis_index("inner")
    z, y = inner // NY, inner % NY
    after = ((outer + 1) % groups, inner)
    before = ((outer + groups - 1) % groups, inner)
    near = sorted(range(1, nz), key=lambda d: (min(d, nz - d), d))
    far = near[::-1]
    place = {d: i for i, d in enumerate([0] + near)}
    ydist = (2, 1, 3)
    mid = nz // 2

    def ypeer(d):
        return (outer, z * NY + (y + d) % NY)

    def zpeer(d):
        return (outer, ((z + d) % nz) * NY + y)

    def at(ref, d, prior=False):
        return ref.at[pl.ds(place[d] * T + (own_rows if prior else 0), T)]

    def cols(ref, h):
        return ref.at[:, pl.ds(h * T, T)]

    def copy_of(kind, h, d):
        if kind in ("k", "v"):
            ref, src, ssem, rsem = (ka, k_in, s_k, r_k) if kind == "k" else (va, v_in, s_v, r_v)
            s, e = h
            return (at(ref, s) if s else src, at(ref, d), ssem.at[d], rsem.at[d], zpeer(e))
        if kind in ("kf", "vf"):
            ref, src, ssem, rsem = (ka, k_in, s_kf, r_k) if kind == "kf" else (va, v_in, s_vf, r_v)
            return (at(ref, d) if d else src, at(ref, d, True), ssem.at[d], rsem.at[nz + d], after)
        if kind == "q":
            return (cols(q_in, h), qa.at[h, pl.ds((NY - d) * T, T)], s_q.at[h, d], r_q.at[h, NY - d], ypeer(d))
        if kind == "g":
            return (cols(g_in, h), ga.at[h, pl.ds((NY - d) * T, T)], s_g.at[h, d], r_g.at[h, NY - d], ypeer(d))
        if kind in ("qr", "gr"):
            ref, ssem, rsem = (qa, s_q, r_q) if kind == "qr" else (ga, s_g, r_g)
            return (ref.at[h, pl.ds((NY - d) * T, T)], ref.at[h, pl.ds(2 * T, T)], ssem.at[h, 2], rsem.at[h, 2], ypeer(d))
        if kind == "stats":
            return (stats.at[h, 0], stats.at[h, NY - d], s_st.at[h, d], r_st.at[h, NY - d], ypeer(d))
        if kind == "delta":
            return (dels.at[h, 0], dels.at[h, NY - d], s_de.at[h, d], r_de.at[h, NY - d], ypeer(d))
        if kind == "dq":
            return (dqb.at[h, d], rdq.at[h, NY - d], s_dq.at[h, d], r_dq.at[h, NY - d], ypeer(d))
        if kind in ("pdv", "pdk"):
            src, dst = (dvacc, pdv) if kind == "pdv" else (dkacc, pdk)
            i = d + (2 if kind == "pdk" else 0)
            return (src.at[pl.ds(own_rows + d * mid * T, mid * T)], dst.at[pl.ds(d * mid * T, mid * T)],
                    s_p.at[i], r_p.at[i], before)
        if kind in ("dvp", "dkp"):
            src, dst, ssem, rsem = (dvp, rdvp, s_dvp, r_dvp) if kind == "dvp" else (dkp, rdkp, s_dkp, r_dkp)
            return (at(src, d), dst.at[(nz - d) % nz], ssem.at[d], rsem.at[(nz - d) % nz],
                    (before[0], ((z + d) % nz) * NY + y))
        if kind == "dv":
            return (at(dvb, d), rdv.at[nz - d], s_dv.at[d], r_dv.at[nz - d], zpeer(d))
        return (at(dkb, d), rdk.at[nz - d], s_dk.at[d], r_dk.at[nz - d], zpeer(d))

    started, received = [], set()

    def remote(key):
        src, dst, ssem, rsem, dev = copy_of(*key)
        return pltpu.make_async_remote_copy(src_ref=src, dst_ref=dst, send_sem=ssem, recv_sem=rsem,
                                            device_id=dev, device_id_type=MESH)

    def start(kind, h=0, ds=(0,)):
        for d in ds:
            started.append((kind, h, d))
            if COMM:
                remote((kind, h, d)).start()

    def recv(kind, h=0, ds=(0,)):
        for d in ds:
            if (kind, h, d) in received:
                continue
            received.add((kind, h, d))
            if COMM:
                remote((kind, h, d)).wait_recv()

    def ring_start(kind, s, steps):
        for e in steps:
            start(kind, (s, e % nz), ((s - e) % nz,))

    def ring_recv(kind, ds):
        for d in ds:
            recv(kind, (0, nz - d), (d,))

    def on_core(core, work):
        if COMM:
            pl.when(outer % 2 == core)(work)
        elif core == 1:
            work()

    def finish():
        if COMM:
            for key in started:
                remote(key).wait_send()

    locals_ = [pltpu.make_async_copy(k_in, at(ka, 0), loc.at[0]), pltpu.make_async_copy(v_in, at(va, 0), loc.at[1])]
    for h in range(heads):
        locals_.append(pltpu.make_async_copy(cols(q_in, h), qa.at[h, pl.ds(0, T)], loc.at[2 + 2 * h]))
        locals_.append(pltpu.make_async_copy(cols(g_in, h), ga.at[h, pl.ds(0, T)], loc.at[3 + 2 * h]))
    for c in locals_:
        c.start()
    if COMM:
        peers = [ypeer(d) for d in BARY] + [zpeer(d) for d in BARZ] + [after, before]
        barrier = pltpu.get_barrier_semaphore()
        for peer in peers:
            pl.semaphore_signal(barrier, inc=1, device_id=peer, device_id_type=MESH)
        pl.semaphore_wait(barrier, len(peers))
    two, six = 2, nz - 2
    ring_start("k", 0, (2, -2, 1, -1))
    start("kf")
    for h in range(heads):
        start("q", h, ydist)

    def start_vg():
        ring_start("v", 0, (2, -2, 1, -1))
        start("vf")
        for h in range(heads):
            start("g", h, (1, 3))

    nst = 2 * NY
    half = T // 2
    lane = lax.broadcasted_iota(jnp.int32, (1, T), 1)
    qorder = jnp.full((1, T), 1 << 20, jnp.int32)
    for s in range(nst):
        block = z * NY + (y + s // 2) % NY
        qorder = jnp.where(lane == s, order[2 * block + s % 2], qorder)
    for d in range(nz):
        block = ((z + d) % nz) * NY + y
        for i in range(2):
            row = jnp.where(order[2 * block + i] > qorder, NEG, 0.0)
            mk[pl.ds(place[d] * T + i * half, half), :] = jnp.broadcast_to(row, (half, T)).astype(BF16)
    first = jnp.where(jnp.logical_and(outer == 0, lane < nst), NEG, 0.0)
    mk[pl.ds(own_rows, own_rows), :] = jnp.broadcast_to(first, (own_rows, T)).astype(BF16)
    sub = lax.broadcasted_iota(jnp.int32, (T, width), 0)
    col = lax.broadcasted_iota(jnp.int32, (T, width), 1)
    onehot = jnp.where(sub == col // half, 1.0, 0.0).astype(BF16)
    for h in range(heads):
        qx[h, pl.ds(T, T), :] = onehot
    o0, o1 = order[2 * inner], order[2 * inner + 1]
    kt_i = lax.broadcasted_iota(jnp.int32, (T, T), 0)
    qt_i = lax.broadcasted_iota(jnp.int32, (T, T), 1)
    kpos = jnp.where(kt_i < half, o0, o1) * half + kt_i % half
    qpos = jnp.where(qt_i < half, o0, o1) * half + qt_i % half
    dvacc[...] = jnp.zeros_like(dvacc)
    dkacc[...] = jnp.zeros_like(dkacc)
    dqt[...] = jnp.zeros_like(dqt)

    for c in locals_:
        c.wait()

    def fold(x):
        return x.reshape(x.shape[0] // 8, 8, width)

    tops, sums = {}, {}

    def pass_a(h, lo, hi):
        lo, hi = lo * T, hi * T
        if lo == 0:
            recv("q", h, ydist)
            qx[h, pl.ds(0, T), :] = qa[h].T
        rows = pl.ds(lo, hi - lo)
        left = jnp.concatenate([ka[rows, :], mk[rows, :]], axis=1)
        s = jnp.dot(left, qx[h], preferred_element_type=F32)
        if lo == 0:
            t = jnp.where(kpos <= qpos, s[:T, :T], NEG)
            s = jnp.concatenate([jnp.concatenate([t, s[:T, T:]], axis=1), s[T:]], axis=0)
        e_buf[h, rows, :] = s
        m = jnp.max(fold(s), axis=0)
        tops8[h] = m if lo == 0 else jnp.maximum(tops8[h], m)

    def exponentials(h):
        top = jnp.max(tops8[h], axis=0, keepdims=True)
        l = jnp.zeros((8, width), F32)
        for i in range(keys // CS):
            rows = pl.ds(i * CS, CS)
            e = jnp.exp2((e_buf[h, rows, :] - top) * cexp)
            e_buf[h, rows, :] = e
            l = l + jnp.sum(fold(e), axis=0)
        stats[h, 0, pl.ds(0, 1), :] = top
        stats[h, 0, pl.ds(1, 1), :] = jnp.sum(l, axis=0, keepdims=True)
        start("stats", h, ydist)

    def prepare(h):
        recv("gr", h, turn(h))
        g = ga[h].T.astype(F32) * scale
        g_hi = g.astype(BF16)
        gx[h, pl.ds(0, T), :] = g_hi
        gx[h, pl.ds(T, T), :] = (g - g_hi.astype(F32)).astype(BF16)

    def dprobs(h, lo):
        rows = pl.ds(lo, own_rows)
        v = va[rows, :]
        d_buf[h, rows, :] = jnp.dot(jnp.concatenate([v, v], axis=1), gx[h], preferred_element_type=F32)

    def turn(h):
        return (3,) if h % 2 == 0 else (1,)

    def each_head(work, h0=0, h1=None):
        h1 = heads if h1 is None else h1
        for h in range(h0, h1):
            work(h)

    def wait_y(kind, h):
        if COMM:
            for d in ydist:
                remote((kind, h, d)).wait_recv()

    def forward(kind, ds):
        ring_recv(kind, ds)
        start(kind + "f", 0, ds)

    def relay(kind):
        for h in range(heads):
            recv(kind, h, (1, 3))
            start(kind + "r", h, turn(h))

    ring_recv("k", (six, two))
    ring_start("k", six, (1,))
    ring_start("k", two, (-1, -2))
    start("kf", 0, (six, two))
    forward("k", (nz - 1, 1))
    start_vg()
    for h in range(heads):
        pass_a(h, 0, 5)
    forward("k", (3, nz - 3, mid))
    ring_recv("v", (six, two))
    ring_start("v", two, (-1,))
    ring_start("v", six, (1, 2))
    relay("g")
    start("vf", 0, (six, two))
    forward("v", (1, nz - 1))
    for h in range(heads):
        pass_a(h, 5, 8)
    recv("kf", 0, (0, 1, nz - 1, two, six))
    for h in range(heads):
        pass_a(h, 8, 13)
    forward("v", (3, nz - 3, mid))
    recv("kf", 0, (3, nz - 3, mid))
    for h in range(heads):
        pass_a(h, 13, 16)
    for h in range(heads):
        exponentials(h)
    for h in range(heads):
        prepare(h)
    for i in range(keys // CD):
        kt[i] = ka[pl.ds(i * CD, CD), :].T
    for h in range(heads):
        dprobs(h, 0)
    recv("vf", 0, [0] + near)
    for h in range(heads):
        dprobs(h, own_rows)

    def aligned(ref, h, r, row):
        part = ref[h, r, pl.ds(row, 1), :]
        if r == 0:
            return part
        cut = (NY - r) * T
        return jnp.concatenate([part[:, cut:], part[:, :cut]], axis=1)

    def second(h):
        wait_y("stats", h)
        parts = [aligned(stats, h, r, 0) for r in range(NY)]
        top = functools.reduce(jnp.maximum, parts)
        weights = [jnp.exp2((t - top) * cexp) for t in parts]
        total = sum(w * aligned(stats, h, r, 1) for r, w in enumerate(weights))
        f = weights[0] * (1.0 / total)
        acc = jnp.zeros((8, width), F32)
        for i in range(keys // CC):
            rows = pl.ds(i * CC, CC)
            p = e_buf[h, rows, :] * f
            e_buf[h, rows, :] = p
            pb = p.astype(BF16)
            dvacc[rows, :] = dvacc[rows, :] + jnp.dot(pb, ga[h], preferred_element_type=F32)
            acc = acc + jnp.sum(fold(pb.astype(F32) * d_buf[h, rows, :]), axis=0)
        dels[h, 0] = jnp.sum(acc, axis=0, keepdims=True)
        if COMM:
            for d in ydist:
                remote(("delta", h, d)).start()

    each_head(second)
    for h in range(heads):
        started.extend([("delta", h, d) for d in ydist])
    own = pl.ds(0, own_rows)
    prior = pl.ds(own_rows, own_rows)

    def each(kind, ds, act):
        if COMM:
            for d in ds:
                getattr(remote((kind, 0, d)), act)()

    @functools.partial(on_core, 0)
    def _():
        dvp[...] = dvacc[prior, :].astype(BF16)
        each("dvp", [0] + far, "start")

    @functools.partial(on_core, 1)
    def _():
        each("pdv", (0, 1), "start")
        dvb[...] = dvacc[own, :].astype(BF16)
        each("dv", far, "start")

    def dq_part(h, d):
        return dqt[h, pl.ds(d * T, T), :] if TN else dqt[h, :, pl.ds(d * T, T)].T

    def third(h, lo, n, first, last):
        if first:
            wait_y("delta", h)
        delta = sum(aligned(dels, h, r, 0) for r in range(NY))
        dq = None
        for i in range(lo * T // CD, (lo + n) * T // CD):
            rows = pl.ds(i * CD, CD)
            ds = (e_buf[h, rows, :] * (d_buf[h, rows, :] - delta)).astype(BF16)
            dkacc[rows, :] = dkacc[rows, :] + jnp.dot(ds, qa[h], preferred_element_type=F32)
            if TN:
                term = lax.dot_general(ds, ka[rows, :], (((0,), (0,)), ((), ())), preferred_element_type=F32)
            else:
                term = jnp.dot(kt[i], ds, preferred_element_type=F32)
            dq = term if dq is None else dq + term
        dqt[h] = dq if first else dqt[h] + dq
        if last:
            for d in ydist:
                dqb[h, d] = dq_part(h, d).astype(BF16)
            if COMM:
                for d in ydist:
                    remote(("dq", h, d)).start()

    def part_of(i):
        return [d for d in [0] + far if place[d] // mid == i]

    def prior_dk(i):
        rows, mine = pl.ds(own_rows + i * mid * T, mid * T), pl.ds(i * mid * T, mid * T)

        @functools.partial(on_core, 0)
        def _():
            dkp[mine, :] = dkacc[rows, :].astype(BF16)
            each("dkp", part_of(i), "start")

        @functools.partial(on_core, 1)
        def _():
            each("pdk", (i,), "start")

    def own_dk(i):
        mine = pl.ds(i * mid * T, mid * T)

        @functools.partial(on_core, 0)
        def _():
            each("pdk", (i,), "wait_recv")
            dkacc[mine, :] = dkacc[mine, :] + pdk[mine, :]

        dkb[mine, :] = dkacc[mine, :].astype(BF16)
        each("dk", [d for d in part_of(i) if d], "start")

    each_head(lambda h: third(h, nz + mid, mid, True, False))
    prior_dk(1)
    each_head(lambda h: third(h, nz, mid, False, False))
    prior_dk(0)

    @functools.partial(on_core, 0)
    def _():
        each("pdv", (0, 1), "wait_recv")
        dvacc[own, :] = dvacc[own, :] + pdv[...]
        dvb[...] = dvacc[own, :].astype(BF16)
        each("dv", far, "start")

    each_head(lambda h: third(h, mid, mid, False, False))
    own_dk(1)
    each_head(lambda h: third(h, 0, mid, False, True))
    own_dk(0)

    me = pl.ds(0, T)
    each("dv", far, "wait_recv")
    dvacc[me, :] = dvacc[me, :] + sum(rdv[d].astype(F32) for d in range(1, nz))
    for h in range(heads):
        wait_y("dq", h)
        dq_out[:, pl.ds(h * T, T)] = (dq_part(h, 0) + sum(rdq[h, d].astype(F32) for d in range(1, NY))).astype(BF16)
    each("dk", far, "wait_recv")
    dkacc[me, :] = dkacc[me, :] + sum(rdk[d].astype(F32) for d in range(1, nz))

    @functools.partial(on_core, 1)
    def _():
        each("dvp", [0] + far, "wait_recv")
        each("dkp", [0] + far, "wait_recv")
        dvacc[me, :] = dvacc[me, :] + sum(rdvp[d].astype(F32) for d in range(nz))
        dkacc[me, :] = dkacc[me, :] + sum(rdkp[d].astype(F32) for d in range(nz))

    dv_out[...] = dvacc[me, :].astype(BF16)
    dk_out[...] = dkacc[me, :].astype(BF16)
    finish()
    each("dv", far, "wait_send")
    each("dk", far, "wait_send")
    for h in range(heads):
        each_y = [remote(("dq", h, d)) for d in ydist]
        for c in each_y if COMM else []:
            c.wait_send()

    @functools.partial(on_core, 0)
    def _():
        each("dvp", [0] + far, "wait_send")
        each("dkp", [0] + far, "wait_send")

    @functools.partial(on_core, 1)
    def _():
        each("pdv", (0, 1), "wait_send")
        each("pdk", (0, 1), "wait_send")


def fused(groups, members, query, key, value, grad_out, stretch_order):
    tokens, dh = key.shape
    heads = query.shape[1] // dh
    nz = members // NY
    own = nz * tokens
    keys, width = 2 * own, NY * tokens
    dma = pltpu.SemaphoreType.DMA
    any_spec = pl.BlockSpec(memory_space=pl.ANY)
    vm = pl.BlockSpec(memory_space=pltpu.VMEM)
    V = pltpu.VMEM
    results = pl.pallas_call(
        functools.partial(kernel, groups, members),
        out_shape=(jax.ShapeDtypeStruct(query.shape, BF16), jax.ShapeDtypeStruct(key.shape, BF16),
                   jax.ShapeDtypeStruct(value.shape, BF16)),
        in_specs=[any_spec] * 4 + [pl.BlockSpec(memory_space=pltpu.SMEM)],
        out_specs=(vm, vm, vm),
        scratch_shapes=[
            V((keys, dh), BF16), V((keys, dh), BF16), V((keys, dh), BF16),
            V((heads, width, dh), BF16), V((heads, width, dh), BF16),
            V((keys // CD, dh, CD), BF16), V((heads, 2 * dh, width), BF16), V((heads, 2 * dh, width), BF16),
            V((heads, keys, width), F32), V((heads, keys, width), F32),
            V((keys, dh), F32), V((keys, dh), F32),
            V((heads, width, dh) if TN else (heads, dh, width), F32),
            V((heads, NY, 2, width), F32), V((heads, NY, 1, width), F32),
            V((heads, 8, width), F32), V((heads, 8, width), F32),
            V((own, dh), BF16), V((own, dh), BF16), V((own, dh), BF16), V((own, dh), BF16),
            V((heads, NY, tokens, dh), BF16),
            V((own, dh), F32), V((own, dh), F32),
            V((nz, tokens, dh), BF16), V((nz, tokens, dh), BF16), V((nz, tokens, dh), BF16), V((nz, tokens, dh), BF16),
            V((heads, NY, tokens, dh), BF16),
            dma((2 + 2 * heads,)),
            dma((nz,)), dma((2 * nz,)), dma((nz,)), dma((2 * nz,)), dma((nz,)), dma((nz,)),
            dma((heads, NY)), dma((heads, NY)), dma((heads, NY)), dma((heads, NY)),
            dma((heads, NY)), dma((heads, NY)), dma((heads, NY)), dma((heads, NY)),
            dma((4,)), dma((4,)),
            dma((nz,)), dma((nz,)), dma((nz,)), dma((nz,)), dma((nz,)), dma((nz,)), dma((nz,)), dma((nz,)),
            dma((heads, NY)), dma((heads, NY)),
        ],
        name="attention_backward",
        compiler_params=pltpu.CompilerParams(
            **(dict(collective_id=0, has_side_effects=True) if COMM else {}), vmem_limit_bytes=60 << 20),
    )(query, key, value, grad_out, stretch_order)
    return results


def solution(mesh):
    groups, members = mesh.shape["outer"], mesh.shape["inner"]
    spec = P(("outer", "inner"), None)
    return jax.shard_map(
        functools.partial(fused, groups, members), mesh=mesh,
        in_specs=(spec, spec, spec, spec, P()), out_specs=(spec, spec, spec), check_vma=False)
```
